512 devices in a mesh: dp: 2 (over core), section: 8 (over y, z_hi), tensor: 32 (over z_lo, x).
Axes of the slice: x: 4, y: 4, z: 16 (z_hi: 2, z_lo: 8; z = z_hi * 8 + z_lo), core: 2. Of those that a mesh axis runs over, the one named last changes fastest.
Arguments:
- layer_saved_input: bfloat16 [8, 1536, 16384], P('section', 'dp', 'tensor'), may hold values from -8 to 8
- key_value_gradient: bfloat16 [8, 1536, 2048], P('section', ('dp', 'tensor')), may hold values from -6 to 6
- key_value_weight: bfloat16 [8, 16384, 2048], P('section', 'tensor'), may hold values from -0.046875 to 0.046875
- adapter_down_weight: bfloat16 [8, 16384, 32], P('section', 'tensor'), may hold values from -0.046875 to 0.046875
- adapter_up_weight: bfloat16 [8, 2, 16, 1024], P('section'), may hold values from -0.1875 to 0.1875
- attention_norm_scale: float32 [8, 16384], P('section', 'tensor'), may hold values from 0.25 to 1.75
Outputs:
- input_grad: bfloat16 [8, 1536, 16384], P('section', 'dp', 'tensor')
- down_grad: float32 [8, 16384, 32], P('section', 'tensor')
- up_grad: float32 [8, 2, 16, 1024], P('section')
The draws below stay inside these ranges and needn't reach their ends.
All inputs are finite; a program needn't handle non-finite values.
Results may differ from the reference program's by a relative error of at most 0.0095.
Values may be sent and summed in bfloat16 or wider, within the bound.
No kernel may reach another device: no remote copies, remote signals or barrier semaphores. Data moves between devices by JAX's collectives and lax.ppermute only.
A program may use at most 128 MiB of HBM per device.

```python
import jax
import jax.numpy as jnp
from jax import lax

MODEL_WIDTH = 16384
KEY_VALUE_WIDTH = 1024
ADAPTER_RANK = 16
TOKEN_COUNT = 1536
WINDOW_LAYERS = 8


def draw_layer_saved_input(key, part):
    key = jax.random.fold_in(key, 7)
    first, second, third = jax.random.split(key, 3)
    position = jnp.arange(MODEL_WIDTH, dtype=jnp.float32) / MODEL_WIDTH
    feature_scale = jnp.exp(jnp.log(3.0) * position) * jax.random.uniform(second, (MODEL_WIDTH,), jnp.float32, 0.6, 1.4)
    token_scale = jax.random.uniform(third, (WINDOW_LAYERS, TOKEN_COUNT, 1), jnp.float32, 0.5, 2.0)
    noise = jax.random.normal(first, (WINDOW_LAYERS, TOKEN_COUNT, MODEL_WIDTH), jnp.float32)
    values = noise * feature_scale[None, None, :] * token_scale
    return jnp.clip(values, -8.0, 8.0).astype(jnp.bfloat16)


def levels(stream_key, extent, shards, least, high):
    def one(axis_at, blocks):
        draws = jax.random.uniform(jax.random.fold_in(jax.random.fold_in(stream_key, 6), axis_at), (blocks,), jnp.float32, least / len(shards), high / len(shards))
        return jnp.repeat(jnp.exp(draws), extent[axis_at] // blocks).reshape((-1,) + (1,) * (len(extent) - axis_at - 1))

    gain = one(*shards[0])
    for cut in shards[1:]:
        gain = gain * one(*cut)
    return gain


def centred(key, extent, spread, bound, shards=(), kind=jnp.bfloat16):
    result = jax.random.normal(key, extent, jnp.float32) * spread
    if len(shards) > 0:
        result = levels(key, extent, shards, -0.22, 0.18) * result
    return jnp.clip(result, min=-bound, max=bound).astype(kind)


def setup_inputs(seed: int = 0) -> dict:
    seeds = jax.random.split(jax.random.key(seed), 7)
    layer_saved_input = draw_layer_saved_input(jax.random.fold_in(seeds[6], 71), 0)
    key_value_gradient = centred(seeds[1], (WINDOW_LAYERS, TOKEN_COUNT, 2 * KEY_VALUE_WIDTH), 1.0, 6.0, ((0, 8), (1, 64)))
    key_value_weight = centred(seeds[2], (WINDOW_LAYERS, MODEL_WIDTH, 2 * KEY_VALUE_WIDTH), MODEL_WIDTH ** -0.5, 0.046875, ((0, 8), (1, 32)))
    adapter_down_weight = centred(seeds[3], (WINDOW_LAYERS, MODEL_WIDTH, 2 * ADAPTER_RANK), MODEL_WIDTH ** -0.5, 0.046875, ((0, 8), (1, 32)))
    adapter_up_weight = centred(seeds[4], (WINDOW_LAYERS, 2, ADAPTER_RANK, KEY_VALUE_WIDTH), KEY_VALUE_WIDTH ** -0.5, 0.1875, ((0, 8),))
    attention_norm_scale = jnp.clip(1.0 + 0.15 * jax.random.normal(seeds[5], (WINDOW_LAYERS, MODEL_WIDTH), jnp.float32), 0.25, 1.75)
    return dict(layer_saved_input=layer_saved_input, key_value_gradient=key_value_gradient, key_value_weight=key_value_weight, adapter_down_weight=adapter_down_weight, adapter_up_weight=adapter_up_weight, attention_norm_scale=attention_norm_scale)


adapter_scale = 2.0
norm_epsilon = 1e-05

def layer_gradient_terms(inputs, kv_grads, weight, down_map, adapter_up_matrix, gain_row, count):
    widened = inputs.astype(jnp.float32)
    inverse = lax.rsqrt(lax.optimization_barrier(jnp.mean(widened * widened, axis=1, keepdims=True)) + norm_epsilon)
    scaled = widened * inverse
    normed = (scaled * gain_row[None, :]).astype(jnp.bfloat16)
    row_count = inputs.shape[0]
    half_width = kv_grads.shape[1] // 2
    grads_three = kv_grads.reshape(row_count, 2, half_width).astype(jnp.float32)
    hidden = jnp.einsum('tck,crk->tcr', grads_three, adapter_up_matrix.astype(jnp.float32))
    hidden = hidden.reshape(row_count, -1).astype(jnp.bfloat16)
    lowered = jnp.dot(normed, down_map, preferred_element_type=jnp.float32).astype(jnp.bfloat16)
    base_term = lax.dot_general(kv_grads, weight, (((1,), (1,)), ((), ())), preferred_element_type=jnp.float32)
    adapter_term = lax.dot_general(hidden, down_map, (((1,), (1,)), ((), ())), preferred_element_type=jnp.float32)
    normed_grad = base_term + adapter_scale * adapter_term
    scaled_grad = normed_grad * gain_row[None, :]
    center = lax.optimization_barrier(jnp.mean(scaled_grad * scaled, axis=1, keepdims=True))
    branch_index = ((scaled_grad - scaled * center) * inverse).astype(jnp.bfloat16)
    factor = adapter_scale / count
    down_gradient_total = factor * lax.dot_general(normed, hidden, (((0,), (0,)), ((), ())), preferred_element_type=jnp.float32)
    lowered_three = lowered.reshape(row_count, 2, -1).astype(jnp.float32)
    up_gradient_total = factor * jnp.einsum('tcr,tck->crk', lowered_three, grads_three)
    return (branch_index, down_gradient_total, up_gradient_total)

def reference(layer_saved_input, key_value_gradient, key_value_weight, adapter_down_weight, adapter_up_weight, attention_norm_scale):
    branches = []
    down_list = []
    up_list = []
    for window_layer_index in range(WINDOW_LAYERS):
        branch_index, down_gradient_total, up_gradient_total = layer_gradient_terms(layer_saved_input[window_layer_index], key_value_gradient[window_layer_index], key_value_weight[window_layer_index], adapter_down_weight[window_layer_index], adapter_up_weight[window_layer_index], attention_norm_scale[window_layer_index], TOKEN_COUNT)
        branches.append(branch_index)
        down_list.append(down_gradient_total)
        up_list.append(up_gradient_total)
    running = jnp.zeros(branches[0].shape, jnp.float32)
    results = [None] * WINDOW_LAYERS
    for window_layer_index in reversed(range(WINDOW_LAYERS)):
        running = running + branches[window_layer_index].astype(jnp.float32)
        results[window_layer_index] = running.astype(jnp.bfloat16)
    return (jnp.stack(results), jnp.stack(down_list), jnp.stack(up_list))
```

```python
import jax
import jax.numpy as jnp
from jax import lax
from jax.sharding import PartitionSpec as P

adapter_scale = 2.0
norm_epsilon = 1e-05
rows_x = 4
rows_z = 8


def swap(value, axis, mask):
    count = lax.axis_size(axis)
    return lax.ppermute(value, axis, [(i, i ^ mask) for i in range(count)])


def ordered(mine, other, bit, axis):
    low = jnp.where(bit, other, mine)
    high = jnp.where(bit, mine, other)
    return jnp.stack([low, high], axis=axis)


def y_pairs(pairs):
    return [(2 * a + z, 2 * b + z) for a, b in pairs for z in range(2)]


def y_scan(value, y):
    first = lax.ppermute(value, "section", y_pairs([(3, 2), (2, 3), (1, 0)]))
    pair = (value.astype(jnp.float32) + first.astype(jnp.float32)).astype(jnp.bfloat16)
    second = lax.ppermute(pair, "section", y_pairs([(2, 1), (3, 0)]))
    return jnp.where(y == 3, 0.0, first.astype(jnp.float32)) + second.astype(jnp.float32)


def local(
    layer_saved_input,
    key_value_gradient,
    key_value_weight,
    adapter_down_weight,
    adapter_up_weight,
    attention_norm_scale,
):
    f32, b16 = jnp.float32, jnp.bfloat16
    x = layer_saved_input[0]
    kv_own = key_value_gradient[0]
    weight = key_value_weight[0]
    down_map = adapter_down_weight[0]
    up_map = adapter_up_weight[0]
    gain = attention_norm_scale[0]
    tokens, span = x.shape
    own, kv_width = kv_own.shape
    half = kv_width // 2
    rank_two = down_map.shape[1]
    rank = rank_two // 2
    width = span * lax.axis_size("tensor")
    factor = adapter_scale / (tokens * lax.axis_size("dp"))
    me = lax.axis_index("tensor")
    section = lax.axis_index("section")
    x_at, z_at = me % rows_x, me // rows_x
    y, zh = section // 2, section % 2

    wide = x.astype(f32)
    square = jnp.sum(wide * wide, axis=1)
    gained = (down_map.astype(f32) * gain[:, None]).astype(b16)
    low = lax.dot_general(gained, x, (((0,), (1,)), ((), ())), preferred_element_type=f32)

    def stats_step(low, square, mask):
        top = square.astype(b16)
        rest = (square - top.astype(f32)).astype(b16)
        got = swap(jnp.concatenate([low.astype(b16), top[None], rest[None]], axis=0), "tensor", mask)
        got = got.astype(f32)
        return low + got[:rank_two], square + (got[rank_two] + got[rank_two + 1])

    have = kv_own
    for depth, bit in enumerate((2, 1, 0)):
        other = swap(have, "tensor", rows_x << bit)
        if depth > 0:
            low, square = stats_step(low, square, (1, 3)[depth - 1])
        have = ordered(have, other, (z_at >> bit) & 1 == 1, depth)
        if depth > 0:
            have, low, square = lax.optimization_barrier((have, low, square))
    have = have.reshape(rows_z, 1, own, kv_width)
    kv_all = jnp.zeros((rows_z, rows_x, own, kv_width), b16)
    kv_all = lax.dynamic_update_slice_in_dim(kv_all, have, x_at, 1)
    parts = [swap(have, "tensor", mask) for mask in (1, 3, 2)]
    for mask in (16, 8, 4):
        low, square = stats_step(low, square, mask)
    inverse = lax.rsqrt(square / width + norm_epsilon)
    lowered = (low * inverse[None, :]).astype(b16)
    parts, inverse, lowered = lax.optimization_barrier((parts, inverse, lowered))
    for mask, part in zip((1, 3, 2), parts):
        kv_all = lax.dynamic_update_slice_in_dim(kv_all, part, x_at ^ mask, 1)
    kv_all = kv_all.reshape(tokens, kv_width)

    base = lax.dot_general(kv_all, weight, (((1,), (1,)), ((), ())), preferred_element_type=f32)
    hidden = jnp.concatenate(
        [
            lax.dot_general(
                kv_all[:, c * half : (c + 1) * half], up_map[c], (((1,), (1,)), ((), ())), preferred_element_type=f32
            )
            for c in range(2)
        ],
        axis=1,
    ).astype(b16)
    adapter = lax.dot_general(hidden, down_map, (((1,), (1,)), ((), ())), preferred_element_type=f32)
    scaled_grad = (base + adapter_scale * adapter) * gain[None, :]
    center = jnp.sum(scaled_grad * wide, axis=1)
    for mask in (1, 3, 4, 8, 16):
        center = center + swap(center, "tensor", mask)
    pull = center * (inverse * inverse / width)
    branch = ((scaled_grad - wide * pull[:, None]) * inverse[:, None]).astype(b16)

    cut = tokens // 2
    early, late = branch[:cut], branch[cut:]
    late_other = swap(late, "section", 1).astype(f32)
    early_tail = y_scan(early, y)
    early_sum = early.astype(f32) + early_tail
    early_send = jnp.where(zh == 1, early_sum, early_tail).astype(b16)
    late_pair = late.astype(f32) + late_other
    late_tail = y_scan(late_pair.astype(b16), y)
    late_out = jnp.where(zh == 0, late_pair, late.astype(f32)) + late_tail
    early_out = early_sum + swap(early_send, "section", 1).astype(f32)
    result = jnp.concatenate([early_out.astype(b16), late_out.astype(b16)], axis=0)

    normed_hidden = (hidden.astype(f32) * inverse[:, None]).astype(b16)
    down = lax.dot_general(x, normed_hidden, (((0,), (0,)), ((), ())), preferred_element_type=f32)
    down = down * (factor * gain[:, None])
    down = down + swap(down, "dp", 1)
    up = factor * jnp.stack(
        [
            jnp.dot(
                lowered[c * rank : (c + 1) * rank],
                kv_all[:, c * half : (c + 1) * half],
                preferred_element_type=f32,
            )
            for c in range(2)
        ]
    )
    up = up + swap(up, "dp", 1)
    return (result[None], down[None], up[None])


def solution(mesh):
    in_specs = (
        P("section", "dp", "tensor"),
        P("section", ("dp", "tensor"), None),
        P("section", "tensor", None),
        P("section", "tensor", None),
        P("section", None, None, None),
        P("section", "tensor"),
    )
    out_specs = (
        P("section", "dp", "tensor"),
        P("section", "tensor", None),
        P("section", None, None, None),
    )
    return jax.shard_map(local, mesh=mesh, in_specs=in_specs, out_specs=out_specs, check_vma=False)
```

```python
import jax
import jax.numpy as jnp
from jax import lax
from jax.sharding import Mesh, PartitionSpec as P

adapter_scale = 2.0
norm_epsilon = 1e-05
sizes = {"dp": 2, "y": 4, "zh": 2, "zl": 8, "x": 4}
section_axes = ("y", "zh")
tensor_axes = ("zl", "x")
together = lax.optimization_barrier


def swap(value, axis, mask):
    count = lax.axis_size(axis)
    return lax.ppermute(value, axis, [(i, i ^ mask) for i in range(count)])


def ordered(mine, other, bit, axis):
    low = jnp.where(bit, other, mine)
    high = jnp.where(bit, mine, other)
    return jnp.stack([low, high], axis=axis)


def y_first(value):
    return lax.ppermute(value, "y", [(3, 2), (2, 3), (1, 0)])


def y_second(value):
    return lax.ppermute(value, "y", [(2, 1), (3, 0)])


def local(
    layer_saved_input,
    key_value_gradient,
    key_value_weight,
    adapter_down_weight,
    adapter_up_weight,
    attention_norm_scale,
):
    f32, b16 = jnp.float32, jnp.bfloat16
    x = layer_saved_input[0]
    kv_own = key_value_gradient[0]
    weight = key_value_weight[0]
    down_map = adapter_down_weight[0]
    up_map = adapter_up_weight[0]
    gain = attention_norm_scale[0]
    tokens, span = x.shape
    own, kv_width = kv_own.shape
    half = kv_width // 2
    rank_two = down_map.shape[1]
    rank = rank_two // 2
    width = span * lax.axis_size(tensor_axes)
    factor = adapter_scale / (tokens * lax.axis_size("dp"))
    x_at, z_at = lax.axis_index("x"), lax.axis_index("zl")
    y, zh = lax.axis_index("y"), lax.axis_index("zh")

    wide = x.astype(f32)
    gained = (down_map.astype(f32) * gain[:, None]).astype(b16)
    low = lax.dot_general(gained, x, (((0,), (1,)), ((), ())), preferred_element_type=f32)

    def low_step(low, axis, mask):
        return low + swap(low.astype(b16), axis, mask).astype(f32)

    kv_all = jnp.zeros((2, 2, 2, sizes["x"], own, kv_width), b16)
    bits = [(z_at >> i) & 1 for i in range(3)]

    def place(kv_all, part, middle, bit, at):
        part = part.reshape((2, -1, 1, 1, own, kv_width))
        return lax.dynamic_update_slice(kv_all, part, (0, middle, bit, at, 0, 0))

    other = swap(kv_own, "zl", 4)
    two = ordered(kv_own, other, bits[2] == 1, 0)
    square = jnp.sum(wide * wide, axis=1)
    two, low, square = together((two, low, square))

    other_two = swap(two, "zl", 2)
    parts = [swap(two, "x", mask) for mask in (2, 1, 3)]
    low = low_step(low, "zl", 4)
    other_two, parts, low = together((other_two, parts, low))
    for mask, part in zip((2, 1, 3), parts):
        kv_all = place(kv_all, part, bits[1], bits[0], x_at ^ mask)
    far = parts[0]

    four = ordered(two, other_two, bits[1] == 1, 1)
    other_four = swap(four, "zl", 1)
    parts = [swap(other_two, "x", mask) for mask in (2, 1, 3)]
    low = low_step(low, "zl", 2)
    other_four, parts, low = together((other_four, parts, low))
    kv_all = place(kv_all, four, 0, bits[0], x_at)
    kv_all = place(kv_all, other_four, 0, 1 - bits[0], x_at)
    for mask, part in zip((2, 1, 3), parts):
        kv_all = place(kv_all, part, 1 - bits[1], bits[0], x_at ^ mask)
    far = ordered(far, parts[0], bits[1] == 1, 1)

    parts = [swap(far, "zl", 1)] + [swap(other_four, "x", mask) for mask in (1, 3)]
    low = low_step(low, "zl", 1)
    parts, low = together((parts, low))
    for mask, part in zip((2, 1, 3), parts):
        kv_all = place(kv_all, part, 0, 1 - bits[0], x_at ^ mask)
    kv_all = kv_all.reshape(tokens, kv_width)

    base = lax.dot_general(kv_all, weight, (((1,), (1,)), ((), ())), preferred_element_type=f32)
    hidden = jnp.concatenate(
        [
            lax.dot_general(
                kv_all[:, c * half : (c + 1) * half], up_map[c], (((1,), (1,)), ((), ())), preferred_element_type=f32
            )
            for c in range(2)
        ],
        axis=1,
    ).astype(b16)
    adapter = lax.dot_general(hidden, down_map, (((1,), (1,)), ((), ())), preferred_element_type=f32)
    scaled_grad = (base + adapter_scale * adapter) * gain[None, :]
    center = jnp.sum(scaled_grad * wide, axis=1)
    square, center = reduce_rows(jnp.stack([square, center]))
    inverse = lax.rsqrt(square / width + norm_epsilon)
    pull = center * (inverse * inverse / width)
    branch = ((scaled_grad - wide * pull[:, None]) * inverse[:, None]).astype(b16)

    cut = tokens // 2
    early, late = branch[:cut], branch[cut:]
    late_other = swap(late, "zh", 1)
    early_one = y_first(early)
    low = low_step(low, "x", 1)
    late_other, early_one, low = together((late_other, early_one, low))
    late_pair = late.astype(f32) + late_other.astype(f32)
    early_pair = early.astype(f32) + early_one.astype(f32)
    early_two = y_second(early_pair.astype(b16))
    late_sent = late_pair.astype(b16)
    late_one = y_first(late_sent)
    low = low_step(low, "x", 3)
    early_two, late_one, low = together((early_two, late_one, low))
    lowered = (low * inverse[None, :]).astype(b16)
    early_tail = jnp.where(y == 3, 0.0, early_one.astype(f32)) + early_two.astype(f32)
    early_sum = early.astype(f32) + early_tail
    early_other = swap(jnp.where(zh == 1, early_sum, early_tail).astype(b16), "zh", 1)
    late_two = y_second((late_sent.astype(f32) + late_one.astype(f32)).astype(b16))
    late_tail = jnp.where(y == 3, 0.0, late_one.astype(f32)) + late_two.astype(f32)
    late_out = jnp.where(zh == 0, late_pair, late.astype(f32)) + late_tail
    early_out = early_sum + early_other.astype(f32)
    result = jnp.concatenate([early_out.astype(b16), late_out.astype(b16)], axis=0)

    normed_hidden = (hidden.astype(f32) * inverse[:, None]).astype(b16)
    down = lax.dot_general(x, normed_hidden, (((0,), (0,)), ((), ())), preferred_element_type=f32)
    down = down * (factor * gain[:, None])
    down = down + swap(down, "dp", 1)
    up = factor * jnp.stack(
        [
            jnp.dot(
                lowered[c * rank : (c + 1) * rank],
                kv_all[:, c * half : (c + 1) * half],
                preferred_element_type=f32,
            )
            for c in range(2)
        ]
    )
    up = up + swap(up, "dp", 1)
    return (result[None], down[None], up[None])


def reduce_rows(rows):
    rows = lax.psum(rows, "x")
    count = sizes["zl"]
    spread = jnp.broadcast_to(rows.reshape(1, -1, 128), (count, rows.size // 128, 128))
    return jnp.sum(lax.all_to_all(spread, "zl", 0, 0), axis=0).reshape(rows.shape)


def solution(mesh):
    mesh = Mesh(mesh.devices.reshape(tuple(sizes.values())), tuple(sizes))
    in_specs = (
        P(section_axes, "dp", tensor_axes),
        P(section_axes, ("dp",) + tensor_axes, None),
        P(section_axes, tensor_axes, None),
        P(section_axes, tensor_axes, None),
        P(section_axes, None, None, None),
        P(section_axes, tensor_axes),
    )
    out_specs = (
        P(section_axes, "dp", tensor_axes),
        P(section_axes, tensor_axes, None),
        P(section_axes, None, None, None),
    )
    return jax.shard_map(local, mesh=mesh, in_specs=in_specs, out_specs=out_specs, check_vma=False)
```

```python
import jax
import jax.numpy as jnp
from jax import lax
from jax.sharding import Mesh, PartitionSpec as P

adapter_scale = 2.0
norm_epsilon = 1e-05
sizes = {"dp": 2, "y": 4, "zh": 2, "zl": 8, "x": 4}
section_axes = ("y", "zh")
tensor_axes = ("zl", "x")
together = lax.optimization_barrier


def swap(value, axis, mask):
    count = lax.axis_size(axis)
    return lax.ppermute(value, axis, [(i, i ^ mask) for i in range(count)])


def ordered(mine, other, bit, axis):
    low = jnp.where(bit, other, mine)
    high = jnp.where(bit, mine, other)
    return jnp.stack([low, high], axis=axis)


def later_y(value):
    count = lax.axis_size("y")
    return [lax.ppermute(value, "y", [(i, i - d) for i in range(d, count)]) for d in range(1, count)]


def local(
    layer_saved_input,
    key_value_gradient,
    key_value_weight,
    adapter_down_weight,
    adapter_up_weight,
    attention_norm_scale,
):
    f32, b16 = jnp.float32, jnp.bfloat16
    x = layer_saved_input[0]
    kv_own = key_value_gradient[0]
    weight = key_value_weight[0]
    down_map = adapter_down_weight[0]
    up_map = adapter_up_weight[0]
    gain = attention_norm_scale[0]
    tokens, span = x.shape
    own, kv_width = kv_own.shape
    half = kv_width // 2
    rank_two = down_map.shape[1]
    rank = rank_two // 2
    width = span * lax.axis_size(tensor_axes)
    factor = adapter_scale / (tokens * lax.axis_size("dp"))
    x_at, z_at = lax.axis_index("x"), lax.axis_index("zl")
    zh = lax.axis_index("zh")

    wide = x.astype(f32)
    gained = (down_map.astype(f32) * gain[:, None]).astype(b16)
    low = lax.dot_general(gained, x, (((0,), (1,)), ((), ())), preferred_element_type=f32)
    lanes = 128
    chunk = kv_width // lanes
    low = low.reshape(rank_two // chunk, chunk, tokens // lanes, lanes)
    low = jnp.swapaxes(low, 1, 2).reshape(-1, kv_width)

    def low_step(low, axis, mask):
        return low + swap(low.astype(b16), axis, mask).astype(f32)

    def both_swap(part, low, axis, mask):
        rows = part.size // kv_width
        got = swap(jnp.concatenate([part.reshape(rows, kv_width), low.astype(b16)]), axis, mask)
        return got[:rows].reshape(part.shape), low + got[rows:].astype(f32)

    kv_all = jnp.zeros((2, 2, 2, sizes["x"], own, kv_width), b16)
    bits = [(z_at >> i) & 1 for i in range(3)]

    def place(kv_all, part, bit, at):
        part = part.reshape((2, 2, 1, 1, own, kv_width))
        return lax.dynamic_update_slice(kv_all, part, (0, 0, bit, at, 0, 0))

    other = swap(kv_own, "zl", 4)
    two = ordered(kv_own, other, bits[2] == 1, 0)
    square = jnp.sum(wide * wide, axis=1)
    two, low, square = together((two, low, square))

    other_two, low = both_swap(two, low, "zl", 2)
    four = ordered(two, other_two, bits[1] == 1, 1)
    four, low = together((four, low))

    other_four, low = both_swap(four, low, "zl", 1)
    parts = [swap(four, "x", mask) for mask in (2, 1, 3)]
    other_four, parts, low = together((other_four, parts, low))
    kv_all = place(kv_all, four, bits[0], x_at)
    kv_all = place(kv_all, other_four, 1 - bits[0], x_at)
    for mask, part in zip((2, 1, 3), parts):
        kv_all = place(kv_all, part, bits[0], x_at ^ mask)

    parts = [swap(parts[0], "zl", 1)] + [swap(other_four, "x", mask) for mask in (1, 3)]
    parts, low = together((parts, low))
    for mask, part in zip((2, 1, 3), parts):
        kv_all = place(kv_all, part, 1 - bits[0], x_at ^ mask)
    kv_all = kv_all.reshape(tokens, kv_width)

    lift = jnp.concatenate(
        [jnp.dot(down_map[:, c * rank : (c + 1) * rank], up_map[c], preferred_element_type=f32) for c in range(2)], axis=1
    )
    weight = (weight.astype(f32) + adapter_scale * lift).astype(b16)
    base = lax.dot_general(kv_all, weight, (((1,), (1,)), ((), ())), preferred_element_type=f32)
    scaled_grad = base * gain[None, :]
    center = jnp.sum(scaled_grad * wide, axis=1)
    rows = reduce_rows(jnp.stack([square, center]))
    low = low_step(low, "zl", 4)
    (square, center), low, kv_all = together((rows, low, kv_all))
    inverse = lax.rsqrt(square / width + norm_epsilon)
    pull = center * (inverse * inverse / width)
    branch = ((scaled_grad - wide * pull[:, None]) * inverse[:, None]).astype(b16)

    cut = tokens // 2
    early, late = branch[:cut], branch[cut:]
    late_other = swap(late, "zh", 1)
    low = low_step(low, "x", 1)
    early, low = together((early, low))
    early_three = later_y(early)
    late_other, early_three, low = together((late_other, early_three, low))
    early_tail = sum(part.astype(f32) for part in early_three)
    early_sum = early.astype(f32) + early_tail
    late_pair = late.astype(f32) + late_other.astype(f32)
    early_other = swap(jnp.where(zh == 1, early_sum, early_tail).astype(b16), "zh", 1)
    low = low_step(low, "x", 3)
    late_sent, low = together((late_pair.astype(b16), low))
    late_three = later_y(late_sent)
    late_tail = sum(part.astype(f32) for part in late_three)
    late_out = (jnp.where(zh == 0, late_pair, late.astype(f32)) + late_tail).astype(b16)
    early_out = (early_sum + early_other.astype(f32)).astype(b16)
    result = lax.dynamic_update_slice(jnp.pad(late_out, ((cut, 0), (0, 0))), early_out, (0, 0))
    low = jnp.swapaxes(low.reshape(rank_two // chunk, tokens // lanes, chunk, lanes), 1, 2).reshape(rank_two, tokens)
    lowered = (low * inverse[None, :]).astype(b16)

    hidden = jnp.concatenate(
        [
            lax.dot_general(
                kv_all[:, c * half : (c + 1) * half], up_map[c], (((1,), (1,)), ((), ())), preferred_element_type=f32
            )
            for c in range(2)
        ],
        axis=1,
    ).astype(b16)
    normed_hidden = (hidden.astype(f32) * inverse[:, None]).astype(b16)
    down = lax.dot_general(x, normed_hidden, (((0,), (0,)), ((), ())), preferred_element_type=f32)
    down = down * (factor * gain[:, None])
    down = down + swap(down, "dp", 1)
    up = factor * jnp.stack(
        [
            jnp.dot(
                lowered[c * rank : (c + 1) * rank],
                kv_all[:, c * half : (c + 1) * half],
                preferred_element_type=f32,
            )
            for c in range(2)
        ]
    )
    up = up + swap(up, "dp", 1)
    return (result[None], down[None], up[None])


def reduce_rows(rows):
    rows = lax.psum(rows, "x")
    spread = jnp.broadcast_to(rows[None], (sizes["zl"],) + rows.shape)
    return jnp.sum(lax.all_to_all(spread, "zl", 0, 0), axis=0)


def solution(mesh):
    mesh = Mesh(mesh.devices.reshape(tuple(sizes.values())), tuple(sizes))
    in_specs = (
        P(section_axes, "dp", tensor_axes),
        P(section_axes, ("dp",) + tensor_axes, None),
        P(section_axes, tensor_axes, None),
        P(section_axes, tensor_axes, None),
        P(section_axes, None, None, None),
        P(section_axes, tensor_axes),
    )
    out_specs = (
        P(section_axes, "dp", tensor_axes),
        P(section_axes, tensor_axes, None),
        P(section_axes, None, None, None),
    )
    return jax.shard_map(local, mesh=mesh, in_specs=in_specs, out_specs=out_specs, check_vma=False)
```

```python
import jax
import jax.numpy as jnp
from jax import lax
from jax.sharding import Mesh, PartitionSpec as P

adapter_scale = 2.0
norm_epsilon = 1e-05
sizes = {"dp": 2, "y": 4, "zh": 2, "zl": 8, "x": 4}
section_axes = ("y", "zh")
tensor_axes = ("zl", "x")
together = lax.optimization_barrier


def swap(value, axis, mask):
    count = lax.axis_size(axis)
    return lax.ppermute(value, axis, [(i, i ^ mask) for i in range(count)])


def ordered(mine, other, bit, axis):
    low = jnp.where(bit, other, mine)
    high = jnp.where(bit, mine, other)
    return jnp.stack([low, high], axis=axis)


def later_y(value):
    count = lax.axis_size("y")
    return [lax.ppermute(value, "y", [(i, i - d) for i in range(d, count)]) for d in range(1, count)]


def local(
    layer_saved_input,
    key_value_gradient,
    key_value_weight,
    adapter_down_weight,
    adapter_up_weight,
    attention_norm_scale,
):
    f32, b16 = jnp.float32, jnp.bfloat16
    x = layer_saved_input[0]
    kv_own = key_value_gradient[0]
    weight = key_value_weight[0]
    down_map = adapter_down_weight[0]
    up_map = adapter_up_weight[0]
    gain = attention_norm_scale[0]
    tokens, span = x.shape
    own, kv_width = kv_own.shape
    half = kv_width // 2
    rank_two = down_map.shape[1]
    rank = rank_two // 2
    width = span * lax.axis_size(tensor_axes)
    factor = adapter_scale / (tokens * lax.axis_size("dp"))
    x_at, z_at = lax.axis_index("x"), lax.axis_index("zl")
    zh = lax.axis_index("zh")

    wide = x.astype(f32)
    gained = (down_map.astype(f32) * gain[:, None]).astype(b16)
    low = lax.dot_general(gained, x, (((0,), (1,)), ((), ())), preferred_element_type=f32)
    lanes = 128
    chunk = kv_width // lanes
    low = low.reshape(rank_two // chunk, chunk, tokens // lanes, lanes)
    low = jnp.swapaxes(low, 1, 2).reshape(-1, kv_width)

    def low_step(low, axis, mask):
        return low + swap(low.astype(b16), axis, mask).astype(f32)

    def both_swap(part, low, axis, mask):
        rows = part.size // kv_width
        got = swap(jnp.concatenate([part.reshape(rows, kv_width), low.astype(b16)]), axis, mask)
        return got[:rows].reshape(part.shape), low + got[rows:].astype(f32)

    kv_all = jnp.zeros((2, 2, 2, sizes["x"], own, kv_width), b16)
    bits = [(z_at >> i) & 1 for i in range(3)]

    def place(kv_all, part, bit, at):
        part = part.reshape((2, 2, 1, 1, own, kv_width))
        return lax.dynamic_update_slice(kv_all, part, (0, 0, bit, at, 0, 0))

    other = swap(kv_own, "zl", 4)
    two = ordered(kv_own, other, bits[2] == 1, 0)
    square = jnp.sum(wide * wide, axis=1)
    two, low, square = together((two, low, square))

    far = swap(two, "x", 2)
    other_two, low = both_swap(two, low, "zl", 2)
    four = ordered(two, other_two, bits[1] == 1, 1)
    four, other_two, far, low = together((four, other_two, far, low))

    other_far = swap(other_two, "x", 2)
    other_four = swap(four, "zl", 1)
    parts = [swap(four, "x", mask) for mask in (1, 3)]
    low = low_step(low, "zl", 4)
    other_far, other_four, parts, low = together((other_far, other_four, parts, low))
    far = ordered(far, other_far, bits[1] == 1, 1)
    kv_all = place(kv_all, four, bits[0], x_at)
    kv_all = place(kv_all, other_four, 1 - bits[0], x_at)
    for mask, part in zip((2, 1, 3), [far] + parts):
        kv_all = place(kv_all, part, bits[0], x_at ^ mask)

    far, low = both_swap(far, low, "zl", 1)
    parts = [swap(other_four, "x", mask) for mask in (1, 3)]
    far, parts, low = together((far, parts, low))
    for mask, part in zip((2, 1, 3), [far] + parts):
        kv_all = place(kv_all, part, 1 - bits[0], x_at ^ mask)
    kv_all = kv_all.reshape(tokens, kv_width)

    lift = jnp.concatenate(
        [jnp.dot(down_map[:, c * rank : (c + 1) * rank], up_map[c], preferred_element_type=f32) for c in range(2)], axis=1
    )
    weight = (weight.astype(f32) + adapter_scale * lift).astype(b16)
    base = lax.dot_general(kv_all, weight, (((1,), (1,)), ((), ())), preferred_element_type=f32)
    scaled_grad = base * gain[None, :]
    center = jnp.sum(scaled_grad * wide, axis=1)
    rows = reduce_rows(jnp.stack([square, center]))
    (square, center), kv_all, low = together((rows, kv_all, low))
    inverse = lax.rsqrt(square / width + norm_epsilon)
    pull = center * (inverse * inverse / width)
    branch = ((scaled_grad - wide * pull[:, None]) * inverse[:, None]).astype(b16)

    cut = tokens // 2
    early, late = branch[:cut], branch[cut:]
    late_other = swap(late, "zh", 1)
    low = low_step(low, "x", 1)
    early, low = together((early, low))
    early_three = later_y(early)
    early_three, low = together((early_three, low))
    early_tail = sum(part.astype(f32) for part in early_three)
    early_sum = early.astype(f32) + early_tail
    early_sent = jnp.where(zh == 1, early_sum, early_tail).astype(b16)
    early_sent, low = together((early_sent, low))
    early_other = swap(early_sent, "zh", 1)
    low = low_step(low, "x", 3)
    late_other, low = together((late_other, low))
    late_pair = late.astype(f32) + late_other.astype(f32)
    late_sent = late_pair.astype(b16)
    late_three = later_y(late_sent)
    late_tail = sum(part.astype(f32) for part in late_three)
    late_out = (jnp.where(zh == 0, late_pair, late.astype(f32)) + late_tail).astype(b16)
    early_out = (early_sum + early_other.astype(f32)).astype(b16)
    result = lax.dynamic_update_slice(jnp.pad(late_out, ((cut, 0), (0, 0))), early_out, (0, 0))
    low = jnp.swapaxes(low.reshape(rank_two // chunk, tokens // lanes, chunk, lanes), 1, 2).reshape(rank_two, tokens)
    lowered = (low * inverse[None, :]).astype(b16)

    hidden = jnp.concatenate(
        [
            lax.dot_general(
                kv_all[:, c * half : (c + 1) * half], up_map[c], (((1,), (1,)), ((), ())), preferred_element_type=f32
            )
            for c in range(2)
        ],
        axis=1,
    ).astype(b16)
    normed_hidden = (hidden.astype(f32) * inverse[:, None]).astype(b16)
    down = lax.dot_general(x, normed_hidden, (((0,), (0,)), ((), ())), preferred_element_type=f32)
    down = down * (factor * gain[:, None])
    down = down + swap(down, "dp", 1)
    up = factor * jnp.stack(
        [
            jnp.dot(
                lowered[c * rank : (c + 1) * rank],
                kv_all[:, c * half : (c + 1) * half],
                preferred_element_type=f32,
            )
            for c in range(2)
        ]
    )
    up = up + swap(up, "dp", 1)
    return (result[None], down[None], up[None])


def reduce_rows(rows):
    rows = lax.psum(rows, "x")
    spread = jnp.broadcast_to(rows[None], (sizes["zl"],) + rows.shape)
    return jnp.sum(lax.all_to_all(spread, "zl", 0, 0), axis=0)


def solution(mesh):
    mesh = Mesh(mesh.devices.reshape(tuple(sizes.values())), tuple(sizes))
    in_specs = (
        P(section_axes, "dp", tensor_axes),
        P(section_axes, ("dp",) + tensor_axes, None),
        P(section_axes, tensor_axes, None),
        P(section_axes, tensor_axes, None),
        P(section_axes, None, None, None),
        P(section_axes, tensor_axes),
    )
    out_specs = (
        P(section_axes, "dp", tensor_axes),
        P(section_axes, tensor_axes, None),
        P(section_axes, None, None, None),
    )
    return jax.shard_map(local, mesh=mesh, in_specs=in_specs, out_specs=out_specs, check_vma=False)
```

```python
import jax
import jax.numpy as jnp
from jax import lax
from jax.sharding import Mesh, PartitionSpec as P

adapter_scale = 2.0
norm_epsilon = 1e-05
sizes = {"dp": 2, "y": 4, "zh": 2, "zl": 8, "x": 4}
section_axes = ("y", "zh")
tensor_axes = ("zl", "x")
together = lax.optimization_barrier


def swap(value, axis, mask):
    count = lax.axis_size(axis)
    return lax.ppermute(value, axis, [(i, i ^ mask) for i in range(count)])


def ordered(mine, other, bit, axis):
    low = jnp.where(bit, other, mine)
    high = jnp.where(bit, mine, other)
    return jnp.stack([low, high], axis=axis)


def later_y(value):
    count = lax.axis_size("y")
    return [lax.ppermute(value, "y", [(i, i - d) for i in range(d, count)]) for d in range(1, count)]


def cross(value, lower):
    pairs = [(2 * y + 1, 2 * y) for y in range(sizes["y"])] + [(2 * y, 2 * y + 1) for y in lower]
    return lax.ppermute(value, section_axes, pairs)


def local(
    layer_saved_input,
    key_value_gradient,
    key_value_weight,
    adapter_down_weight,
    adapter_up_weight,
    attention_norm_scale,
):
    f32, b16 = jnp.float32, jnp.bfloat16
    x = layer_saved_input[0]
    kv_own = key_value_gradient[0]
    weight = key_value_weight[0]
    down_map = adapter_down_weight[0]
    up_map = adapter_up_weight[0]
    gain = attention_norm_scale[0]
    tokens, span = x.shape
    own, kv_width = kv_own.shape
    half = kv_width // 2
    rank_two = down_map.shape[1]
    rank = rank_two // 2
    width = span * lax.axis_size(tensor_axes)
    factor = adapter_scale / (tokens * lax.axis_size("dp"))
    x_at, z_at = lax.axis_index("x"), lax.axis_index("zl")
    zh = lax.axis_index("zh")

    wide = x.astype(f32)
    gained = (down_map.astype(f32) * gain[:, None]).astype(b16)
    low = lax.dot_general(gained, x, (((0,), (1,)), ((), ())), preferred_element_type=f32)
    lanes = 128
    chunk = kv_width // lanes
    low = low.reshape(rank_two // chunk, chunk, tokens // lanes, lanes)
    low = jnp.swapaxes(low, 1, 2).reshape(-1, kv_width)

    def low_step(low, axis, mask):
        return low + swap(low.astype(b16), axis, mask).astype(f32)

    def both_swap(part, low, axis, mask):
        rows = part.size // kv_width
        got = swap(jnp.concatenate([part.reshape(rows, kv_width), low.astype(b16)]), axis, mask)
        return got[:rows].reshape(part.shape), low + got[rows:].astype(f32)

    kv_all = jnp.zeros((2, 2, 2, sizes["x"], own, kv_width), b16)
    bits = [(z_at >> i) & 1 for i in range(3)]

    def place(kv_all, part, bit, at):
        part = part.reshape((2, 2, 1, 1, own, kv_width))
        return lax.dynamic_update_slice(kv_all, part, (0, 0, bit, at, 0, 0))

    other = swap(kv_own, "zl", 4)
    two = ordered(kv_own, other, bits[2] == 1, 0)
    square = jnp.sum(wide * wide, axis=1)
    two, low, square = together((two, low, square))

    far = swap(two, "x", 2)
    other_two, low = both_swap(two, low, "zl", 2)
    four = ordered(two, other_two, bits[1] == 1, 1)
    four, other_two, far, low = together((four, other_two, far, low))

    other_far = swap(other_two, "x", 2)
    other_four = swap(four, "zl", 1)
    parts = [swap(four, "x", mask) for mask in (1, 3)]
    low = low_step(low, "zl", 4)
    other_far, other_four, parts, low = together((other_far, other_four, parts, low))
    far = ordered(far, other_far, bits[1] == 1, 1)
    kv_all = place(kv_all, four, bits[0], x_at)
    kv_all = place(kv_all, other_four, 1 - bits[0], x_at)
    for mask, part in zip((2, 1, 3), [far] + parts):
        kv_all = place(kv_all, part, bits[0], x_at ^ mask)

    far, low = both_swap(far, low, "zl", 1)
    parts = [swap(other_four, "x", mask) for mask in (1, 3)]
    far, parts, low = together((far, parts, low))
    for mask, part in zip((2, 1, 3), [far] + parts):
        kv_all = place(kv_all, part, 1 - bits[0], x_at ^ mask)
    kv_all = kv_all.reshape(tokens, kv_width)

    lift = jnp.concatenate(
        [jnp.dot(down_map[:, c * rank : (c + 1) * rank], up_map[c], preferred_element_type=f32) for c in range(2)], axis=1
    )
    weight = (weight.astype(f32) + adapter_scale * lift).astype(b16)
    base = lax.dot_general(kv_all, weight, (((1,), (1,)), ((), ())), preferred_element_type=f32)
    scaled_grad = base * gain[None, :]
    center = jnp.sum(scaled_grad * wide, axis=1)
    rows = reduce_rows(jnp.stack([square, center]))
    (square, center), kv_all, low = together((rows, kv_all, low))
    inverse = lax.rsqrt(square / width + norm_epsilon)
    pull = center * (inverse * inverse / width)
    branch = ((scaled_grad - wide * pull[:, None]) * inverse[:, None]).astype(b16)

    cut = tokens // 2
    early, late = branch[:cut], branch[cut:]
    late_other = cross(late, range(1, sizes["y"]))
    low = low_step(low, "x", 1)
    early, low = together((early, low))
    early_three = later_y(early)
    early_three, low = together((early_three, low))
    early_tail = sum(part.astype(f32) for part in early_three)
    early_sum = early.astype(f32) + early_tail
    early_sent = jnp.where(zh == 1, early_sum, early_tail).astype(b16)
    early_sent, low = together((early_sent, low))
    early_other = cross(early_sent, range(sizes["y"] - 1))
    low = low_step(low, "x", 3)
    late_other, low = together((late_other, low))
    late_pair = late.astype(f32) + late_other.astype(f32)
    late_sent = late_pair.astype(b16)
    late_three = later_y(late_sent)
    late_tail = sum(part.astype(f32) for part in late_three)
    late_out = (jnp.where(zh == 0, late_pair, late.astype(f32)) + late_tail).astype(b16)
    early_out = (early_sum + early_other.astype(f32)).astype(b16)
    result = lax.dynamic_update_slice(jnp.pad(late_out, ((cut, 0), (0, 0))), early_out, (0, 0))
    low = jnp.swapaxes(low.reshape(rank_two // chunk, tokens // lanes, chunk, lanes), 1, 2).reshape(rank_two, tokens)
    lowered = (low * inverse[None, :]).astype(b16)

    hidden = jnp.concatenate(
        [
            lax.dot_general(
                kv_all[:, c * half : (c + 1) * half], up_map[c], (((1,), (1,)), ((), ())), preferred_element_type=f32
            )
            for c in range(2)
        ],
        axis=1,
    ).astype(b16)
    normed_hidden = (hidden.astype(f32) * inverse[:, None]).astype(b16)
    down = lax.dot_general(x, normed_hidden, (((0,), (0,)), ((), ())), preferred_element_type=f32)
    down = down * (factor * gain[:, None])
    down = down + swap(down, "dp", 1)
    up = factor * jnp.stack(
        [
            jnp.dot(
                lowered[c * rank : (c + 1) * rank],
                kv_all[:, c * half : (c + 1) * half],
                preferred_element_type=f32,
            )
            for c in range(2)
        ]
    )
    up = up + swap(up, "dp", 1)
    return (result[None], down[None], up[None])


def reduce_rows(rows):
    rows = lax.psum(rows, "x")
    spread = jnp.broadcast_to(rows[None], (sizes["zl"],) + rows.shape)
    return jnp.sum(lax.all_to_all(spread, "zl", 0, 0), axis=0)


def solution(mesh):
    mesh = Mesh(mesh.devices.reshape(tuple(sizes.values())), tuple(sizes))
    in_specs = (
        P(section_axes, "dp", tensor_axes),
        P(section_axes, ("dp",) + tensor_axes, None),
        P(section_axes, tensor_axes, None),
        P(section_axes, tensor_axes, None),
        P(section_axes, None, None, None),
        P(section_axes, tensor_axes),
    )
    out_specs = (
        P(section_axes, "dp", tensor_axes),
        P(section_axes, tensor_axes, None),
        P(section_axes, None, None, None),
    )
    return jax.shard_map(local, mesh=mesh, in_specs=in_specs, out_specs=out_specs, check_vma=False)
```

```python
import jax
import jax.numpy as jnp
from jax import lax
from jax.sharding import Mesh, PartitionSpec as P

adapter_scale = 2.0
norm_epsilon = 1e-05
sizes = {"dp": 2, "y": 4, "zh": 2, "zl": 8, "x": 4}
section_axes = ("y", "zh")
tensor_axes = ("zl", "x")
together = lax.optimization_barrier


def swap(value, axis, mask):
    count = lax.axis_size(axis)
    return lax.ppermute(value, axis, [(i, i ^ mask) for i in range(count)])


def ordered(mine, other, bit, axis):
    low = jnp.where(bit, other, mine)
    high = jnp.where(bit, mine, other)
    return jnp.stack([low, high], axis=axis)


def later_y(value):
    count = lax.axis_size("y")
    return [lax.ppermute(value, "y", [(i, i - d) for i in range(d, count)]) for d in range(1, count)]


def local(
    layer_saved_input,
    key_value_gradient,
    key_value_weight,
    adapter_down_weight,
    adapter_up_weight,
    attention_norm_scale,
):
    f32, b16 = jnp.float32, jnp.bfloat16
    x = layer_saved_input[0]
    kv_own = key_value_gradient[0]
    weight = key_value_weight[0]
    down_map = adapter_down_weight[0]
    up_map = adapter_up_weight[0]
    gain = attention_norm_scale[0]
    tokens, span = x.shape
    own, kv_width = kv_own.shape
    half = kv_width // 2
    rank_two = down_map.shape[1]
    rank = rank_two // 2
    width = span * lax.axis_size(tensor_axes)
    factor = adapter_scale / (tokens * lax.axis_size("dp"))
    x_at, z_at = lax.axis_index("x"), lax.axis_index("zl")
    zh = lax.axis_index("zh")

    wide = x.astype(f32)
    gained = (down_map.astype(f32) * gain[:, None]).astype(b16)
    low = lax.dot_general(gained, x, (((0,), (1,)), ((), ())), preferred_element_type=f32)
    lanes = 128
    chunk = kv_width // lanes
    low = low.reshape(rank_two // chunk, chunk, tokens // lanes, lanes)
    low = jnp.swapaxes(low, 1, 2).reshape(-1, kv_width)

    def low_step(low, axis, mask):
        return low + swap(low.astype(b16), axis, mask).astype(f32)

    def both_swap(part, low, axis, mask):
        rows = part.size // kv_width
        got = swap(jnp.concatenate([part.reshape(rows, kv_width), low.astype(b16)]), axis, mask)
        return got[:rows].reshape(part.shape), low + got[rows:].astype(f32)

    kv_all = jnp.zeros((2, 2, 2, sizes["x"], own, kv_width), b16)
    bits = [(z_at >> i) & 1 for i in range(3)]

    def place(kv_all, part, bit, at):
        part = part.reshape((2, 2, 1, 1, own, kv_width))
        return lax.dynamic_update_slice(kv_all, part, (0, 0, bit, at, 0, 0))

    other = swap(kv_own, "zl", 4)
    two = ordered(kv_own, other, bits[2] == 1, 0)
    square = jnp.sum(wide * wide, axis=1)
    two, low, square = together((two, low, square))

    far = swap(two, "x", 2)
    other_two, low = both_swap(two, low, "zl", 2)
    four = ordered(two, other_two, bits[1] == 1, 1)
    four, other_two, far, low = together((four, other_two, far, low))

    other_far = swap(other_two, "x", 2)
    other_four = swap(four, "zl", 1)
    parts = [swap(four, "x", mask) for mask in (1, 3)]
    low = low_step(low, "zl", 4)
    other_far, other_four, parts, low = together((other_far, other_four, parts, low))
    far = ordered(far, other_far, bits[1] == 1, 1)
    kv_all = place(kv_all, four, bits[0], x_at)
    kv_all = place(kv_all, other_four, 1 - bits[0], x_at)
    for mask, part in zip((2, 1, 3), [far] + parts):
        kv_all = place(kv_all, part, bits[0], x_at ^ mask)

    far, low = both_swap(far, low, "zl", 1)
    parts = [swap(other_four, "x", mask) for mask in (1, 3)]
    far, parts, low = together((far, parts, low))
    for mask, part in zip((2, 1, 3), [far] + parts):
        kv_all = place(kv_all, part, 1 - bits[0], x_at ^ mask)
    kv_all = kv_all.reshape(tokens, kv_width)

    lift = jnp.concatenate(
        [jnp.dot(down_map[:, c * rank : (c + 1) * rank], up_map[c], preferred_element_type=f32) for c in range(2)], axis=1
    )
    weight = (weight.astype(f32) + adapter_scale * lift).astype(b16)
    base = lax.dot_general(kv_all, weight, (((1,), (1,)), ((), ())), preferred_element_type=f32)
    scaled_grad = base * gain[None, :]
    center = jnp.sum(scaled_grad * wide, axis=1)
    rows = reduce_rows(jnp.stack([square, center]))
    (square, center), kv_all, low = together((rows, kv_all, low))
    inverse = lax.rsqrt(square / width + norm_epsilon)
    pull = center * (inverse * inverse / width)
    branch = ((scaled_grad - wide * pull[:, None]) * inverse[:, None]).astype(b16)

    cut = tokens // 2
    early, late = branch[:cut], branch[cut:]
    late_other = swap(late, "zh", 1)
    low = low_step(low, "x", 1)
    early, low = together((early, low))
    early_three = later_y(early)
    early_three, low = together((early_three, low))
    early_tail = sum(part.astype(f32) for part in early_three)
    early_sum = early.astype(f32) + early_tail
    early_sent = jnp.where(zh == 1, early_sum, early_tail).astype(b16)
    early_sent, low = together((early_sent, low))
    early_other = swap(early_sent, "zh", 1)
    low = low_step(low, "x", 3)
    late_other, low = together((late_other, low))
    late_pair = late.astype(f32) + late_other.astype(f32)
    late_sent = late_pair.astype(b16)
    late_three = later_y(late_sent)
    late_tail = sum(part.astype(f32) for part in late_three)
    late_out = (jnp.where(zh == 0, late_pair, late.astype(f32)) + late_tail).astype(b16)
    early_out = (early_sum + early_other.astype(f32)).astype(b16)
    result = lax.dynamic_update_slice(jnp.pad(late_out, ((cut, 0), (0, 0))), early_out, (0, 0))
    low = jnp.swapaxes(low.reshape(rank_two // chunk, tokens // lanes, chunk, lanes), 1, 2).reshape(rank_two, tokens)
    lowered = (low * inverse[None, :]).astype(b16)

    hidden = jnp.concatenate(
        [
            lax.dot_general(
                kv_all[:, c * half : (c + 1) * half], up_map[c], (((1,), (1,)), ((), ())), preferred_element_type=f32
            )
            for c in range(2)
        ],
        axis=1,
    ).astype(b16)
    normed_hidden = (hidden.astype(f32) * inverse[:, None]).astype(b16)
    down = lax.dot_general(x, normed_hidden, (((0,), (0,)), ((), ())), preferred_element_type=f32)
    down = down * (factor * gain[:, None])
    down = down + swap(down, "dp", 1)
    up = factor * jnp.stack(
        [
            jnp.dot(
                lowered[c * rank : (c + 1) * rank],
                kv_all[:, c * half : (c + 1) * half],
                preferred_element_type=f32,
            )
            for c in range(2)
        ]
    )
    up = up + swap(up, "dp", 1)
    return (result[None], down[None], up[None])


def reduce_rows(rows):
    spread = jnp.broadcast_to(rows[None], (sizes["zl"],) + rows.shape)
    return lax.psum(jnp.sum(lax.all_to_all(spread, "zl", 0, 0), axis=0), "x")


def solution(mesh):
    mesh = Mesh(mesh.devices.reshape(tuple(sizes.values())), tuple(sizes))
    in_specs = (
        P(section_axes, "dp", tensor_axes),
        P(section_axes, ("dp",) + tensor_axes, None),
        P(section_axes, tensor_axes, None),
        P(section_axes, tensor_axes, None),
        P(section_axes, None, None, None),
        P(section_axes, tensor_axes),
    )
    out_specs = (
        P(section_axes, "dp", tensor_axes),
        P(section_axes, tensor_axes, None),
        P(section_axes, None, None, None),
    )
    return jax.shard_map(local, mesh=mesh, in_specs=in_specs, out_specs=out_specs, check_vma=False)
```
